32 devices in a mesh: bank: 4 (over y, core), gal: 8 (over z, x).
Axes of the slice: x: 2, y: 2, z: 4, core: 2. Of those that a mesh axis runs over, the one named last changes fastest.
Arguments:
- querybank: bfloat16 [4096, 512], P(('bank', 'gal')), may hold values from -80 to 80
- gallery: bfloat16 [32768, 512], P('gal'), may hold values from -80 to 80
- test_queries: bfloat16 [512, 512], P(('bank', 'gal')), may hold values from -80 to 80
Outputs:
- retrieval: float32 [512, 8, 4096], P(None, 'gal', 'bank')
The draws below stay inside these ranges and needn't reach their ends.
All inputs are finite; a program needn't handle non-finite values.
Results may differ from the reference program's by a relative error of at most 0.0017.
Values may be sent and summed in bfloat16 or wider, within the bound.
No kernel may reach another device: no remote copies, remote signals or barrier semaphores. Data moves between devices by JAX's collectives and lax.ppermute only.
A program may use at most 64 MiB of HBM per device.

```python
import math
import jax
import jax.numpy as jnp
from jax import lax

D = 512
CLIP_GAL = 4096
CLIPS = 32768
BANK = 4096
TESTQ = 512
N_BANK = 4
N_GAL = 8


def embed_rows(key, row_count, tag):
    topics = max(BANK // 64, 4)
    shared = jax.random.fold_in(key, 5)
    centre_key, column_key = jax.random.split(shared)
    row_key = jax.random.fold_in(key, tag)
    pick_key, noise_key, mixing_key, scale_key = jax.random.split(row_key, 4)
    topic_ids = jax.random.randint(pick_key, (row_count,), 0, topics)
    centroids = jax.random.truncated_normal(centre_key, -3.0, 3.0, (topics, D), jnp.float32)
    col_scale = jnp.exp(jax.random.uniform(column_key, (1, D), jnp.float32, math.log(0.5), math.log(2.0)))
    noise_part = jax.random.truncated_normal(noise_key, -3.0, 3.0, (row_count, D), jnp.float32)
    mixing = jax.random.uniform(mixing_key, (row_count, 1), jnp.float32, 0.5, 1.1)
    row_scale = jnp.exp(jax.random.uniform(scale_key, (row_count, 1), jnp.float32, 0.0, math.log(6.0)))
    base_rows = mixing * jnp.take(centroids, topic_ids, axis=0) + noise_part
    return (base_rows * row_scale * col_scale).astype(jnp.bfloat16)


def draw_querybank(key, part):
    return embed_rows(key, BANK, 11)


def draw_gallery(key, part):
    return embed_rows(key, CLIPS, 23)


def draw_test_queries(key, part):
    return embed_rows(key, TESTQ, 37)


def setup_inputs(seed: int = 0) -> dict:
    key_list = jax.random.split(jax.random.key(seed), 4)
    querybank = draw_querybank(jax.random.fold_in(key_list[3], 71), 0)
    gallery = draw_gallery(jax.random.fold_in(key_list[3], 71), 0)
    test_queries = draw_test_queries(jax.random.fold_in(key_list[3], 71), 0)
    return dict(querybank=querybank, gallery=gallery, test_queries=test_queries)


inverse_temp = 20.0
epsilon = 1e-06

def unit_rows(values):
    wide = values.astype(jnp.float32)
    return (wide * lax.rsqrt(lax.optimization_barrier(jnp.sum(wide * wide, axis=-1, keepdims=True)) + epsilon)).astype(jnp.bfloat16)

def reference(querybank, gallery, test_queries):
    captions = unit_rows(querybank).reshape(N_BANK, BANK // N_BANK, D)
    clips = unit_rows(gallery).reshape(N_GAL, CLIP_GAL, D)
    tests = unit_rows(test_queries)

    def per_shard(block):
        block_t = block.T

        def per_group(group):
            sims = jnp.dot(group, block_t, preferred_element_type=jnp.float32)
            return lax.optimization_barrier(jnp.sum(jnp.exp(inverse_temp * sims), axis=0))
        normalizer = lax.optimization_barrier(jnp.sum(lax.map(per_group, captions), axis=0))
        scores = jnp.dot(tests, block_t, preferred_element_type=jnp.float32)
        return inverse_temp * scores - jnp.log(normalizer / BANK)[None, :]
    shards = lax.map(per_shard, clips)
    return jnp.transpose(shards, (1, 0, 2))
```

```python
import functools

import jax
import jax.numpy as jnp
from jax import lax
from jax.experimental import pallas as pl
from jax.experimental.pallas import tpu as pltpu
from jax.sharding import PartitionSpec as P

inverse_temp = 20.0
epsilon = 1e-06
log2_e = 1.4426950408889634
vmem_bytes = 32 * 1024 * 1024


def unit_rows(values):
    wide = values.astype(jnp.float32)
    return (wide * lax.rsqrt(jnp.sum(wide * wide, axis=-1, keepdims=True) + epsilon)).astype(
        jnp.bfloat16
    )


def exp_sums(captions, clips):
    sims = lax.dot_general(
        captions, clips, (((1,), (1,)), ((), ())), preferred_element_type=jnp.float32
    )
    grown = jnp.exp2(sims * (inverse_temp * log2_e))
    return jnp.sum(grown.reshape(grown.shape[0] // 8, 8, grown.shape[1]), axis=0)


def params():
    return pltpu.CompilerParams(vmem_limit_bytes=vmem_bytes)


def prepare(captions, tests):
    rows, more, width = captions.shape[0], tests.shape[0], captions.shape[1]

    def kernel(captions_ref, tests_ref, out_ref):
        out_ref[:rows, :] = unit_rows(captions_ref[...])
        out_ref[rows:, :] = unit_rows(tests_ref[...])

    return pl.pallas_call(
        kernel,
        out_shape=jax.ShapeDtypeStruct((rows + more, width), jnp.bfloat16),
        compiler_params=params(),
        name="prepare",
    )(captions, tests)


def first_sums(bank, gallery, payload, rows, share):
    clips, width = gallery.shape
    block = share // 2

    def kernel(bank_ref, gallery_ref, payload_ref, unit_ref, sums_ref):
        unit = unit_rows(gallery_ref[...])
        unit_ref[...] = unit
        sums_ref[...] = exp_sums(payload_ref[...], unit)

    return pl.pallas_call(
        kernel,
        grid_spec=pltpu.PrefetchScalarGridSpec(
            num_scalar_prefetch=1,
            grid=(clips // block,),
            in_specs=[
                pl.BlockSpec((block, width), lambda j, b: (((j // 2) ^ b[0]) * 2 + j % 2, 0)),
                pl.BlockSpec((rows, width), lambda j, b: (0, 0)),
            ],
            out_specs=[
                pl.BlockSpec((block, width), lambda j, b: (j, 0)),
                pl.BlockSpec((8, block), lambda j, b: (0, j)),
            ],
        ),
        out_shape=[
            jax.ShapeDtypeStruct((clips, width), jnp.bfloat16),
            jax.ShapeDtypeStruct((8, clips), jnp.float32),
        ],
        cost_estimate=pl.CostEstimate(
            flops=2 * rows * clips * width, bytes_accessed=4 * clips * width, transcendentals=0
        ),
        compiler_params=params(),
        name="first_sums",
    )(bank, gallery, payload)


def more_sums(unit, payloads, sums, rows, share):
    clips, width = unit.shape
    block = share // 2
    count = len(payloads)

    def kernel(unit_ref, *refs):
        total = refs[count][...]
        for ref in refs[:count]:
            total = total + exp_sums(ref[...], unit_ref[...])
        refs[count + 1][...] = total

    return pl.pallas_call(
        kernel,
        grid=(clips // block,),
        in_specs=[pl.BlockSpec((block, width), lambda j: (j, 0))]
        + [pl.BlockSpec((rows, width), lambda j: (0, 0))] * count
        + [pl.BlockSpec((8, block), lambda j: (0, j))],
        out_specs=pl.BlockSpec((8, block), lambda j: (0, j)),
        out_shape=jax.ShapeDtypeStruct((8, clips), jnp.float32),
        cost_estimate=pl.CostEstimate(
            flops=2 * rows * clips * width * count, bytes_accessed=2 * clips * width, transcendentals=0
        ),
        compiler_params=params(),
        name="more_sums",
    )(unit, *payloads, sums)


def last_sums(gal, unit, payloads, sums, every, rows, share):
    clips, width = unit.shape
    count, n = len(payloads), len(every)
    more = every[0].shape[0] - rows

    def kernel(gal_ref, unit_ref, *refs):
        step = pl.program_id(0)
        keep_ref, send_ref, tests_ref = refs[count + 1 + n :]
        total = refs[count][...]
        for ref in refs[:count]:
            total = total + exp_sums(ref[...], unit_ref[...])
        total = jnp.sum(total, axis=0, keepdims=True)

        @pl.when(step % 2 == 0)
        def even():
            keep_ref[pl.ds(step // 2, 1), :] = total

        @pl.when(step % 2 == 1)
        def odd():
            send_ref[pl.ds(step // 2, 1), :] = total

        @pl.when(step == 0)
        def tests():
            for mask in range(n):
                place = pl.multiple_of((gal_ref[0] ^ mask) * more, more)
                tests_ref[pl.ds(place, more), :] = refs[count + 1 + mask][...]

    half = clips // share // 2
    return pl.pallas_call(
        kernel,
        grid_spec=pltpu.PrefetchScalarGridSpec(
            num_scalar_prefetch=1,
            grid=(clips // share,),
            in_specs=[pl.BlockSpec((share, width), lambda j, g: (j, 0))]
            + [pl.BlockSpec((rows, width), lambda j, g: (0, 0))] * count
            + [pl.BlockSpec((8, share), lambda j, g: (0, j))]
            + [pl.BlockSpec((more, width), lambda j, g: (rows // more, 0))] * n,
            out_specs=[
                pl.BlockSpec((half, share), lambda j, g: (0, 0)),
                pl.BlockSpec((half, share), lambda j, g: (0, 0)),
                pl.BlockSpec((n * more, width), lambda j, g: (0, 0)),
            ],
        ),
        out_shape=[
            jax.ShapeDtypeStruct((half, share), jnp.float32),
            jax.ShapeDtypeStruct((half, share), jnp.float32),
            jax.ShapeDtypeStruct((n * more, width), jnp.bfloat16),
        ],
        cost_estimate=pl.CostEstimate(
            flops=2 * rows * clips * width * count, bytes_accessed=2 * clips * width, transcendentals=0
        ),
        compiler_params=params(),
        name="last_sums",
    )(gal, unit, *payloads, sums, *every)


def scores(bank, unit, tests, parts, total_count, share):
    width = unit.shape[1]
    rows = tests[0].shape[0]
    lanes = 128
    per_row = share // lanes
    n = len(tests)

    def kernel(bank_ref, unit_ref, *refs):
        out_ref = refs[-1]
        step = pl.program_id(0)
        norm = refs[n][0:1, :] + refs[n + 1][0:1, :] + refs[n + 2][...]
        shift = jnp.log(norm / total_count)
        for which in range(n):

            @pl.when(step == which)
            def one(which=which):
                sims = lax.dot_general(
                    refs[which][...],
                    unit_ref[...],
                    (((1,), (1,)), ((), ())),
                    preferred_element_type=jnp.float32,
                )
                values = inverse_temp * sims - shift
                for k in range(per_row):
                    out_ref[pl.ds(k, rows, stride=per_row), :] = values[:, k * lanes : (k + 1) * lanes]

    return pl.pallas_call(
        kernel,
        grid_spec=pltpu.PrefetchScalarGridSpec(
            num_scalar_prefetch=1,
            grid=(n,),
            in_specs=[pl.BlockSpec((share, width), lambda i, b: (0, 0))]
            + [pl.BlockSpec((rows, width), lambda i, b: (0, 0))] * n
            + [pl.BlockSpec(part.shape, lambda i, b: (0, 0)) for part in parts],
            out_specs=pl.BlockSpec((rows * per_row, lanes), lambda i, b: (i ^ b[0], 0)),
        ),
        out_shape=jax.ShapeDtypeStruct((n * rows * per_row, lanes), jnp.float32),
        cost_estimate=pl.CostEstimate(
            flops=2 * n * rows * share * width, bytes_accessed=4 * n * rows * share, transcendentals=0
        ),
        compiler_params=params(),
        name="scores",
    )(bank, unit, *tests, *parts)


def swap(values, axis, mask):
    size = lax.axis_size(axis)
    return lax.ppermute(values, axis, [(i, i ^ mask) for i in range(size)])


def local(querybank, gallery, test_queries):
    groups, shards = lax.axis_size("bank"), lax.axis_size("gal")
    rows = querybank.shape[0]
    share = gallery.shape[0] // groups
    bank = lax.axis_index("bank").astype(jnp.int32)[None]
    gal = lax.axis_index("gal").astype(jnp.int32)[None]

    payload = prepare(querybank, test_queries)
    low = shards // 4
    got = {0: payload}
    for high in (2, 3, 1):
        got[high * low] = swap(payload, "gal", high * low)
    for mask in range(1, low):
        got[mask] = swap(payload, "gal", mask)
        got[low + mask] = swap(payload, "gal", low + mask)
    for high in (2, 3):
        for mask in range(1, low):
            got[high * low + mask] = swap(got[high * low], "gal", mask)

    unit, sums = first_sums(bank, gallery, payload, rows, share)
    sums = more_sums(unit, [got[m] for m in range(1, 2 * low)], sums, rows, share)
    sums = more_sums(unit, [got[2 * low], got[3 * low]], sums, rows, share)
    last = [got[h * low + m] for h in (2, 3) for m in range(1, low)]
    keep, send, tests = last_sums(
        gal, unit, last, sums, [got[m] for m in range(shards)], rows, share
    )

    tests_y = swap(tests, "bank", 2)
    tests_core = swap(tests, "bank", 1)
    received = swap(send, "bank", 1)
    far = swap(keep[1:] + received[1:], "bank", 2)
    tests_both = swap(tests_y, "bank", 1)
    result = scores(
        bank,
        unit,
        [tests, tests_core, tests_y, tests_both],
        [keep, received, far],
        rows * shards * groups,
        share,
    )
    return result.reshape(-1, 1, share)


def solution(mesh):
    placed = (P(("bank", "gal"), None), P("gal", None), P(("bank", "gal"), None))
    return jax.shard_map(
        local, mesh=mesh, in_specs=placed, out_specs=P(None, "gal", "bank"), check_vma=False
    )
```

```python
import jax
import jax.numpy as jnp
from jax import lax
from jax.experimental import pallas as pl
from jax.experimental.pallas import tpu as pltpu
from jax.sharding import PartitionSpec as P

inverse_temp = 20.0
epsilon = 1e-06
log2_e = 1.4426950408889634
lanes = 128
in_vmem = pl.BlockSpec(memory_space=pltpu.VMEM)
in_smem = pl.BlockSpec(memory_space=pltpu.SMEM)
in_hbm = pl.BlockSpec(memory_space=pltpu.HBM)


def unit_rows(values):
    wide = values.astype(jnp.float32)
    return (wide * lax.rsqrt(jnp.sum(wide * wide, axis=-1, keepdims=True) + epsilon)).astype(
        jnp.bfloat16
    )


def products(left, right):
    return lax.dot_general(
        left, right, (((1,), (1,)), ((), ())), preferred_element_type=jnp.float32
    )


def exp_sums(captions, clips):
    grown = jnp.exp2(products(captions, clips) * (inverse_temp * log2_e))
    return jnp.sum(grown.reshape(grown.shape[0] // 8, 8, grown.shape[1]), axis=0)


def call(kernel, name, out_shape, flops, moved, *args, in_specs, out_specs=in_vmem, scratch=()):
    return pl.pallas_call(
        kernel,
        out_shape=out_shape,
        in_specs=in_specs,
        out_specs=out_specs,
        scratch_shapes=list(scratch),
        cost_estimate=pl.CostEstimate(flops=flops, bytes_accessed=moved, transcendentals=0),
        compiler_params=pltpu.CompilerParams(vmem_limit_bytes=32 * 1024 * 1024),
        name=name,
    )(*args)


def stay_in_hbm(values):
    return pltpu.with_memory_space_constraint(values, pltpu.HBM)


def prepare(captions, tests):
    rows, more, width = captions.shape[0], tests.shape[0], captions.shape[1]

    def kernel(captions_ref, tests_ref, out_ref, captions_in, tests_in, sems):
        first = pltpu.make_async_copy(captions_ref, captions_in, sems.at[0])
        second = pltpu.make_async_copy(tests_ref, tests_in, sems.at[1])
        first.start()
        second.start()
        second.wait()
        out_ref[rows:, :] = unit_rows(tests_in[...])
        first.wait()
        out_ref[:rows, :] = unit_rows(captions_in[...])

    return call(
        kernel,
        "prepare",
        jax.ShapeDtypeStruct((rows + more, width), jnp.bfloat16),
        rows * width,
        rows * width * 4,
        stay_in_hbm(captions),
        stay_in_hbm(tests),
        in_specs=[in_hbm] * 2,
        scratch=[
            pltpu.VMEM(captions.shape, captions.dtype),
            pltpu.VMEM(tests.shape, tests.dtype),
            pltpu.SemaphoreType.DMA((2,)),
        ],
    )


def unit_gallery(bank, gallery, share):
    clips, width = gallery.shape
    quarters = clips // share

    def kernel(bank_ref, gallery_ref, out_ref, arrived, sems):
        half = share // 2
        copies = []
        for k in range(2 * quarters):
            begin = pl.multiple_of(((k // 2) ^ bank_ref[0]) * share + k % 2 * half, half)
            copies.append(
                pltpu.make_async_copy(gallery_ref.at[pl.ds(begin, half)], arrived.at[k], sems.at[k])
            )
            copies[k].start()
        for k in range(2 * quarters):
            copies[k].wait()
            out_ref[k * half : (k + 1) * half, :] = unit_rows(arrived[k])

    return call(
        kernel,
        "unit_gallery",
        jax.ShapeDtypeStruct((clips, width), jnp.bfloat16),
        4 * clips * width,
        4 * clips * width,
        bank,
        stay_in_hbm(gallery),
        in_specs=[in_smem, in_hbm],
        scratch=[
            pltpu.VMEM((2 * quarters, share // 2, width), gallery.dtype),
            pltpu.SemaphoreType.DMA((2 * quarters,)),
        ],
    )


def first_sums(unit, payloads, rows):
    clips, width = unit.shape
    count = len(payloads)

    def kernel(unit_ref, *refs):
        captions = jnp.concatenate([ref[:rows, :] for ref in refs[:count]], axis=0)
        refs[count][...] = exp_sums(captions, unit_ref[...])

    return call(
        kernel,
        "first_sums",
        jax.ShapeDtypeStruct((8, clips), jnp.float32),
        2 * rows * clips * width * count,
        2 * clips * width,
        unit,
        *payloads,
        in_specs=[in_vmem] * (count + 1),
    )


def last_sums(unit, payloads, sums, rows, share):
    clips, width = unit.shape
    count, parts = len(payloads), len(sums)
    half = clips // share // 2

    def kernel(unit_ref, *refs):
        captions = jnp.concatenate([ref[:rows, :] for ref in refs[:count]], axis=0)
        total = exp_sums(captions, unit_ref[...])
        for ref in refs[count : count + parts]:
            total = total + ref[...]
        total = jnp.sum(total, axis=0, keepdims=True)
        keep_ref, send_ref = refs[count + parts :]
        for k in range(half):
            keep_ref[k : k + 1, :] = total[:, 2 * k * share : (2 * k + 1) * share]
            send_ref[k : k + 1, :] = total[:, (2 * k + 1) * share : (2 * k + 2) * share]

    return call(
        kernel,
        "last_sums",
        [jax.ShapeDtypeStruct((half, share), jnp.float32)] * 2,
        2 * rows * clips * width * count,
        2 * clips * width,
        unit,
        *payloads,
        *sums,
        in_specs=[in_vmem] * (1 + count + parts),
        out_specs=[in_vmem] * 2,
    )


def gather_tests(gal, payloads, rows):
    total, width = payloads[0].shape
    more, count = total - rows, len(payloads)

    def kernel(gal_ref, *refs):
        for mask in range(count):
            place = pl.multiple_of((gal_ref[0] ^ mask) * more, more)
            refs[count][pl.ds(place, more), :] = refs[mask][rows:, :]

    return call(
        kernel,
        "gather_tests",
        jax.ShapeDtypeStruct((count * more, width), jnp.bfloat16),
        0,
        4 * count * more * width,
        gal,
        *payloads,
        in_specs=[in_smem] + [in_vmem] * count,
    )


def raw_scores(unit, tests, share):
    rows, width = tests[0].shape
    count = len(tests)

    def kernel(unit_ref, *refs):
        every = jnp.concatenate([ref[...] for ref in refs[:count]], axis=0)
        refs[count][...] = inverse_temp * products(every, unit_ref[:share, :])

    return call(
        kernel,
        "raw_scores",
        jax.ShapeDtypeStruct((count * rows, share), jnp.float32),
        2 * count * rows * share * width,
        4 * count * rows * share,
        unit,
        *tests,
        in_specs=[in_vmem] * (1 + count),
    )


def write_scores(bank, raw, keep, received, far, groups, total):
    every, share = raw.shape
    rows, per_row = every // groups, share // lanes

    def kernel(bank_ref, raw_ref, keep_ref, received_ref, far_ref, out_ref, staged, sems):
        normalizer = keep_ref[0:1, :] + received_ref[0:1, :] + far_ref[...]
        shift = jnp.log(normalizer / total)
        copies = []
        for mask in range(groups):
            values = raw_ref[mask * rows : (mask + 1) * rows, :] - shift
            for k in range(per_row):
                staged[mask, pl.ds(k, rows, stride=per_row), :] = values[:, k * lanes : (k + 1) * lanes]
            begin = pl.multiple_of((bank_ref[0] ^ mask) * (rows * per_row), rows * per_row)
            copies.append(
                pltpu.make_async_copy(
                    staged.at[mask], out_ref.at[pl.ds(begin, rows * per_row)], sems.at[mask]
                )
            )
            copies[mask].start()
        for copy in copies:
            copy.wait()

    return call(
        kernel,
        "write_scores",
        jax.ShapeDtypeStruct((every * per_row, lanes), jnp.float32),
        every * share,
        8 * every * share,
        bank,
        raw,
        keep,
        received,
        far,
        in_specs=[in_smem] + [in_vmem] * 4,
        out_specs=in_hbm,
        scratch=[
            pltpu.VMEM((groups, rows * per_row, lanes), jnp.float32),
            pltpu.SemaphoreType.DMA((groups,)),
        ],
    )


def swap(values, axis, mask):
    size = lax.axis_size(axis)
    return lax.ppermute(values, axis, [(i, i ^ mask) for i in range(size)])


def after(values, other):
    return lax.optimization_barrier((values, other))[0]


def local(querybank, gallery, test_queries):
    groups, shards = lax.axis_size("bank"), lax.axis_size("gal")
    rows = querybank.shape[0]
    share = gallery.shape[0] // groups
    bank = lax.axis_index("bank").astype(jnp.int32)[None]
    gal = lax.axis_index("gal").astype(jnp.int32)[None]

    payload = prepare(querybank, test_queries)
    low = shards // 4
    got = {0: payload}
    for high in (2, 3, 1):
        got[high * low] = swap(payload, "gal", high * low)
    for mask in range(1, low):
        got[low + mask] = swap(payload, "gal", low + mask)
        got[mask] = swap(payload, "gal", mask)

    unit = unit_gallery(bank, gallery, share)
    sums = [first_sums(unit, [got[m] for m in range(2 * low)], rows)]
    for high in (2, 3):
        here = after(got[high * low], sums[0])
        for mask in range(1, low):
            got[high * low + mask] = swap(here, "gal", mask)
    sums.append(first_sums(unit, [got[2 * low], got[3 * low]], rows))

    for high in (2, 3):
        for mask in range(1, low):
            got[high * low + mask] = after(got[high * low + mask], sums[1])
    tests = gather_tests(gal, [got[m] for m in range(shards)], rows)
    tests_y = swap(tests, "bank", 2)
    tests_core = swap(tests, "bank", 1)
    last = [got[h * low + m] for h in (2, 3) for m in range(1, low)]
    keep, send = last_sums(unit, last, sums, rows, share)
    received = swap(send, "bank", 1)
    far = swap(keep[1:] + received[1:], "bank", 2)
    tests_both = swap(after(tests_y, received), "bank", 1)
    raw = raw_scores(unit, [tests, tests_core, tests_y, tests_both], share)
    result = write_scores(bank, raw, keep, received, far, groups, rows * shards * groups)
    return result.reshape(-1, 1, share)


def solution(mesh):
    placed = (P(("bank", "gal"), None), P("gal", None), P(("bank", "gal"), None))
    return jax.shard_map(
        local, mesh=mesh, in_specs=placed, out_specs=P(None, "gal", "bank"), check_vma=False
    )
```

```python
import jax
import jax.numpy as jnp
from jax import lax
from jax.experimental import pallas as pl
from jax.experimental.pallas import tpu as pltpu
from jax.sharding import PartitionSpec as P

inverse_temp = 20.0
epsilon = 1e-06
log2_e = 1.4426950408889634
lanes = 128
in_vmem = pl.BlockSpec(memory_space=pltpu.VMEM)
in_smem = pl.BlockSpec(memory_space=pltpu.SMEM)
in_hbm = pl.BlockSpec(memory_space=pltpu.HBM)


def unit_rows(values):
    wide = values.astype(jnp.float32)
    return (wide * lax.rsqrt(jnp.sum(wide * wide, axis=-1, keepdims=True) + epsilon)).astype(
        jnp.bfloat16
    )


def products(left, right):
    return lax.dot_general(
        left, right, (((1,), (1,)), ((), ())), preferred_element_type=jnp.float32
    )


def exp_sums(captions, clips):
    grown = jnp.exp2(products(captions, clips) * (inverse_temp * log2_e))
    return jnp.sum(grown.reshape(grown.shape[0] // 8, 8, grown.shape[1]), axis=0)


def call(kernel, name, out_shape, flops, moved, *args, in_specs, out_specs=in_vmem, scratch=()):
    return pl.pallas_call(
        kernel,
        out_shape=out_shape,
        in_specs=in_specs,
        out_specs=out_specs,
        scratch_shapes=list(scratch),
        cost_estimate=pl.CostEstimate(flops=flops, bytes_accessed=moved, transcendentals=0),
        compiler_params=pltpu.CompilerParams(vmem_limit_bytes=32 * 1024 * 1024),
        name=name,
    )(*args)


def stay_in_hbm(values):
    return pltpu.with_memory_space_constraint(values, pltpu.HBM)


def prepare(captions, tests):
    rows, more, width = captions.shape[0], tests.shape[0], captions.shape[1]

    def kernel(captions_ref, tests_ref, out_ref, captions_in, tests_in, sems):
        first = pltpu.make_async_copy(captions_ref, captions_in, sems.at[0])
        second = pltpu.make_async_copy(tests_ref, tests_in, sems.at[1])
        first.start()
        second.start()
        second.wait()
        out_ref[rows:, :] = unit_rows(tests_in[...])
        first.wait()
        out_ref[:rows, :] = unit_rows(captions_in[...])

    return call(
        kernel,
        "prepare",
        jax.ShapeDtypeStruct((rows + more, width), jnp.bfloat16),
        rows * width,
        rows * width * 4,
        stay_in_hbm(captions),
        stay_in_hbm(tests),
        in_specs=[in_hbm] * 2,
        scratch=[
            pltpu.VMEM(captions.shape, captions.dtype),
            pltpu.VMEM(tests.shape, tests.dtype),
            pltpu.SemaphoreType.DMA((2,)),
        ],
    )


def normalize(captions):
    rows, width = captions.shape

    def kernel(captions_ref, out_ref):
        out_ref[...] = unit_rows(captions_ref[...])

    return call(
        kernel,
        "normalize",
        jax.ShapeDtypeStruct((rows, width), jnp.bfloat16),
        10**9,
        4 * rows * width,
        captions,
        in_specs=[in_vmem],
    )


def unit_gallery(bank, gallery, share):
    clips, width = gallery.shape
    quarters = clips // share

    def kernel(bank_ref, gallery_ref, out_ref, arrived, sems):
        half = share // 2
        copies = []
        for k in range(2 * quarters):
            begin = pl.multiple_of(((k // 2) ^ bank_ref[0]) * share + k % 2 * half, half)
            copies.append(
                pltpu.make_async_copy(gallery_ref.at[pl.ds(begin, half)], arrived.at[k], sems.at[k])
            )
            copies[k].start()
        for k in range(2 * quarters):
            copies[k].wait()
            out_ref[k * half : (k + 1) * half, :] = unit_rows(arrived[k])

    return call(
        kernel,
        "unit_gallery",
        jax.ShapeDtypeStruct((clips, width), jnp.bfloat16),
        4 * clips * width,
        4 * clips * width,
        bank,
        stay_in_hbm(gallery),
        in_specs=[in_smem, in_hbm],
        scratch=[
            pltpu.VMEM((2 * quarters, share // 2, width), gallery.dtype),
            pltpu.SemaphoreType.DMA((2 * quarters,)),
        ],
    )


def first_sums(unit, payloads, raw, rows):
    clips, width = unit.shape
    done = len(payloads)
    payloads = payloads + raw
    count = len(payloads)

    def kernel(unit_ref, *refs):
        captions = jnp.concatenate(
            [ref[:rows, :] for ref in refs[:done]] + [unit_rows(ref[...]) for ref in refs[done:count]],
            axis=0,
        )
        refs[count][...] = exp_sums(captions, unit_ref[...])

    return call(
        kernel,
        "first_sums",
        jax.ShapeDtypeStruct((8, clips), jnp.float32),
        2 * rows * clips * width * count,
        2 * clips * width,
        unit,
        *payloads,
        in_specs=[in_vmem] * (count + 1),
    )


def last_sums(unit, raw, sums, rows, share):
    clips, width = unit.shape
    count, parts = len(raw), len(sums)
    half = clips // share // 2

    def kernel(unit_ref, *refs):
        captions = jnp.concatenate([ref[...] for ref in refs[:count]], axis=0)
        total = exp_sums(captions, unit_ref[...])
        for ref in refs[count : count + parts]:
            total = total + ref[...]
        total = jnp.sum(total, axis=0, keepdims=True)
        keep_ref, send_ref = refs[count + parts :]
        for k in range(half):
            keep_ref[k : k + 1, :] = total[:, 2 * k * share : (2 * k + 1) * share]
            send_ref[k : k + 1, :] = total[:, (2 * k + 1) * share : (2 * k + 2) * share]

    return call(
        kernel,
        "last_sums",
        [jax.ShapeDtypeStruct((half, share), jnp.float32)] * 2,
        2 * rows * clips * width * count,
        2 * clips * width,
        unit,
        *raw,
        *sums,
        in_specs=[in_vmem] * (1 + count + parts),
        out_specs=[in_vmem] * 2,
    )


def near_tests(gal, payloads, rows):
    total, width = payloads[0].shape
    more, count = total - rows, len(payloads)

    def kernel(gal_ref, *refs):
        for mask in range(count):
            place = pl.multiple_of(((gal_ref[0] ^ mask) % count) * more, more)
            refs[count][pl.ds(place, more), :] = refs[mask][rows:, :]

    return call(
        kernel,
        "near_tests",
        jax.ShapeDtypeStruct((count * more, width), jnp.bfloat16),
        0,
        4 * count * more * width,
        gal,
        *payloads,
        in_specs=[in_smem] + [in_vmem] * count,
    )


def all_tests(gal, near, far, near_count):
    rows, width = near.shape

    def kernel(gal_ref, near_ref, far_ref, out_ref):
        half = (gal_ref[0] // near_count) % 2
        out_ref[pl.ds(pl.multiple_of(half * rows, rows), rows), :] = near_ref[...]
        out_ref[pl.ds(pl.multiple_of((1 - half) * rows, rows), rows), :] = far_ref[...]

    return call(
        kernel,
        "all_tests",
        jax.ShapeDtypeStruct((2 * rows, width), jnp.bfloat16),
        0,
        8 * rows * width,
        gal,
        near,
        far,
        in_specs=[in_smem] + [in_vmem] * 2,
    )


def raw_scores(unit, tests, share):
    rows, width = tests[0].shape
    count = len(tests)

    def kernel(unit_ref, *refs):
        every = jnp.concatenate([ref[...] for ref in refs[:count]], axis=0)
        refs[count][...] = inverse_temp * products(every, unit_ref[:share, :])

    return call(
        kernel,
        "raw_scores",
        jax.ShapeDtypeStruct((count * rows, share), jnp.float32),
        2 * count * rows * share * width,
        4 * count * rows * share,
        unit,
        *tests,
        in_specs=[in_vmem] * (1 + count),
    )


def write_scores(bank, raw, keep, received, far, groups, total):
    every, share = raw.shape
    rows, per_row = every // groups, share // lanes

    def kernel(bank_ref, raw_ref, keep_ref, received_ref, far_ref, out_ref, staged, sems):
        normalizer = keep_ref[0:1, :] + received_ref[0:1, :] + far_ref[...]
        shift = jnp.log(normalizer / total)
        copies = []
        for mask in range(groups):
            values = raw_ref[mask * rows : (mask + 1) * rows, :] - shift
            for k in range(per_row):
                staged[mask, pl.ds(k, rows, stride=per_row), :] = values[:, k * lanes : (k + 1) * lanes]
            begin = pl.multiple_of((bank_ref[0] ^ mask) * (rows * per_row), rows * per_row)
            copies.append(
                pltpu.make_async_copy(
                    staged.at[mask], out_ref.at[pl.ds(begin, rows * per_row)], sems.at[mask]
                )
            )
            copies[mask].start()
        for copy in copies:
            copy.wait()

    return call(
        kernel,
        "write_scores",
        jax.ShapeDtypeStruct((every * per_row, lanes), jnp.float32),
        every * share,
        8 * every * share,
        bank,
        raw,
        keep,
        received,
        far,
        in_specs=[in_smem] + [in_vmem] * 4,
        out_specs=in_hbm,
        scratch=[
            pltpu.VMEM((groups, rows * per_row, lanes), jnp.float32),
            pltpu.SemaphoreType.DMA((groups,)),
        ],
    )


def swap(values, axis, mask):
    size = lax.axis_size(axis)
    return lax.ppermute(values, axis, [(i, i ^ mask) for i in range(size)])


def after(values, other):
    return lax.optimization_barrier((values, other))[0]


def local(querybank, gallery, test_queries):
    groups, shards = lax.axis_size("bank"), lax.axis_size("gal")
    rows = querybank.shape[0]
    share = gallery.shape[0] // groups
    bank = lax.axis_index("bank").astype(jnp.int32)[None]
    gal = lax.axis_index("gal").astype(jnp.int32)[None]

    half = shards // 2
    across = normalize(swap(querybank, "gal", half))
    payload = prepare(querybank, test_queries)
    near = [payload] + [swap(payload, "gal", mask) for mask in range(1, half)]

    unit = unit_gallery(bank, gallery, share)
    here = near_tests(gal, [near[0]] + [after(x, across) for x in near[1:]], rows)
    there = swap(here, "gal", half)
    last = [swap(across, "gal", mask) for mask in range(1, half)]
    sums = [first_sums(unit, near, [], rows)]

    tests = all_tests(gal, here, there, half)
    tests_y = swap(tests, "bank", 2)
    tests_core = swap(tests, "bank", 1)
    tests_both = swap(tests_y, "bank", 1)
    raw = raw_scores(unit, [tests, tests_core, tests_y, tests_both], share)

    keep, send = last_sums(unit, [across] + last, sums, rows, share)
    received = swap(send, "bank", 1)
    other = swap(keep[1:] + received[1:], "bank", 2)
    result = write_scores(bank, raw, keep, received, other, groups, rows * shards * groups)
    return result.reshape(-1, 1, share)


def solution(mesh):
    placed = (P(("bank", "gal"), None), P("gal", None), P(("bank", "gal"), None))
    return jax.shard_map(
        local, mesh=mesh, in_specs=placed, out_specs=P(None, "gal", "bank"), check_vma=False
    )
```

```python
import jax
import jax.numpy as jnp
from jax import lax
from jax.experimental import pallas as pl
from jax.experimental.pallas import tpu as pltpu
from jax.sharding import PartitionSpec as P

inverse_temp = 20.0
epsilon = 1e-06
log2_e = 1.4426950408889634
lanes = 128
in_vmem = pl.BlockSpec(memory_space=pltpu.VMEM)
in_smem = pl.BlockSpec(memory_space=pltpu.SMEM)
in_hbm = pl.BlockSpec(memory_space=pltpu.HBM)


def unit_rows(values):
    wide = values.astype(jnp.float32)
    return (wide * lax.rsqrt(jnp.sum(wide * wide, axis=-1, keepdims=True) + epsilon)).astype(
        jnp.bfloat16
    )


def products(left, right):
    return lax.dot_general(
        left, right, (((1,), (1,)), ((), ())), preferred_element_type=jnp.float32
    )


def exp_sums(captions, clips):
    grown = jnp.exp2(products(captions, clips) * (inverse_temp * log2_e))
    return jnp.sum(grown.reshape(grown.shape[0] // 8, 8, grown.shape[1]), axis=0)


def call(kernel, name, out_shape, flops, moved, *args, in_specs, out_specs=in_vmem, scratch=()):
    return pl.pallas_call(
        kernel,
        out_shape=out_shape,
        in_specs=in_specs,
        out_specs=out_specs,
        scratch_shapes=list(scratch),
        cost_estimate=pl.CostEstimate(flops=flops, bytes_accessed=moved, transcendentals=0),
        compiler_params=pltpu.CompilerParams(vmem_limit_bytes=32 * 1024 * 1024),
        name=name,
    )(*args)


def stay_in_hbm(values):
    return pltpu.with_memory_space_constraint(values, pltpu.HBM)


def prepare(captions, tests):
    rows, more, width = captions.shape[0], tests.shape[0], captions.shape[1]

    def kernel(captions_ref, tests_ref, out_ref, captions_in, tests_in, sems):
        first = pltpu.make_async_copy(captions_ref, captions_in, sems.at[0])
        second = pltpu.make_async_copy(tests_ref, tests_in, sems.at[1])
        first.start()
        second.start()
        second.wait()
        out_ref[rows:, :] = unit_rows(tests_in[...])
        first.wait()
        out_ref[:rows, :] = unit_rows(captions_in[...])

    return call(
        kernel,
        "prepare",
        jax.ShapeDtypeStruct((rows + more, width), jnp.bfloat16),
        rows * width,
        rows * width * 4,
        stay_in_hbm(captions),
        stay_in_hbm(tests),
        in_specs=[in_hbm] * 2,
        scratch=[
            pltpu.VMEM(captions.shape, captions.dtype),
            pltpu.VMEM(tests.shape, tests.dtype),
            pltpu.SemaphoreType.DMA((2,)),
        ],
    )


def normalize(captions):
    rows, width = captions.shape

    def kernel(captions_ref, out_ref):
        out_ref[...] = unit_rows(captions_ref[...])

    return call(
        kernel,
        "normalize",
        jax.ShapeDtypeStruct((rows, width), jnp.bfloat16),
        10**9,
        4 * rows * width,
        captions,
        in_specs=[in_vmem],
    )


def unit_gallery(bank, gallery, share):
    clips, width = gallery.shape
    quarters = clips // share

    def kernel(bank_ref, gallery_ref, out_ref, arrived, sems):
        half = share // 2
        copies = []
        for k in range(2 * quarters):
            begin = pl.multiple_of(((k // 2) ^ bank_ref[0]) * share + k % 2 * half, half)
            copies.append(
                pltpu.make_async_copy(gallery_ref.at[pl.ds(begin, half)], arrived.at[k], sems.at[k])
            )
            copies[k].start()
        for k in range(2 * quarters):
            copies[k].wait()
            out_ref[k * half : (k + 1) * half, :] = unit_rows(arrived[k])

    return call(
        kernel,
        "unit_gallery",
        jax.ShapeDtypeStruct((clips, width), jnp.bfloat16),
        4 * clips * width,
        4 * clips * width,
        bank,
        stay_in_hbm(gallery),
        in_specs=[in_smem, in_hbm],
        scratch=[
            pltpu.VMEM((2 * quarters, share // 2, width), gallery.dtype),
            pltpu.SemaphoreType.DMA((2 * quarters,)),
        ],
    )


def first_sums(unit, payloads, raw, rows):
    clips, width = unit.shape
    done = len(payloads)
    payloads = payloads + raw
    count = len(payloads)

    def kernel(unit_ref, *refs):
        captions = jnp.concatenate(
            [ref[:rows, :] for ref in refs[:done]] + [unit_rows(ref[...]) for ref in refs[done:count]],
            axis=0,
        )
        refs[count][...] = exp_sums(captions, unit_ref[...])

    return call(
        kernel,
        "first_sums",
        jax.ShapeDtypeStruct((8, clips), jnp.float32),
        2 * rows * clips * width * count,
        2 * clips * width,
        unit,
        *payloads,
        in_specs=[in_vmem] * (count + 1),
    )


def last_sums(unit, raw, sums, rows, share):
    clips, width = unit.shape
    count, parts = len(raw), len(sums)
    half = clips // share // 2

    def kernel(unit_ref, *refs):
        captions = jnp.concatenate([ref[...] for ref in refs[:count]], axis=0)
        total = exp_sums(captions, unit_ref[...])
        for ref in refs[count : count + parts]:
            total = total + ref[...]
        total = jnp.sum(total, axis=0, keepdims=True)
        keep_ref, send_ref = refs[count + parts :]
        for k in range(half):
            keep_ref[k : k + 1, :] = total[:, k * share : (k + 1) * share]
            send_ref[k : k + 1, :] = total[:, (half + k) * share : (half + k + 1) * share]

    return call(
        kernel,
        "last_sums",
        [jax.ShapeDtypeStruct((half, share), jnp.float32)] * 2,
        2 * rows * clips * width * count,
        2 * clips * width,
        unit,
        *raw,
        *sums,
        in_specs=[in_vmem] * (1 + count + parts),
        out_specs=[in_vmem] * 2,
    )


def near_tests(gal, payloads, rows):
    total, width = payloads[0].shape
    more, count = total - rows, len(payloads)

    def kernel(gal_ref, *refs):
        for mask in range(count):
            place = pl.multiple_of(((gal_ref[0] ^ mask) % count) * more, more)
            refs[count][pl.ds(place, more), :] = refs[mask][rows:, :]

    return call(
        kernel,
        "near_tests",
        jax.ShapeDtypeStruct((count * more, width), jnp.bfloat16),
        0,
        4 * count * more * width,
        gal,
        *payloads,
        in_specs=[in_smem] + [in_vmem] * count,
    )


def all_tests(gal, near, far, near_count):
    rows, width = near.shape

    def kernel(gal_ref, near_ref, far_ref, out_ref):
        half = (gal_ref[0] // near_count) % 2
        out_ref[pl.ds(pl.multiple_of(half * rows, rows), rows), :] = near_ref[...]
        out_ref[pl.ds(pl.multiple_of((1 - half) * rows, rows), rows), :] = far_ref[...]

    return call(
        kernel,
        "all_tests",
        jax.ShapeDtypeStruct((2 * rows, width), jnp.bfloat16),
        0,
        8 * rows * width,
        gal,
        near,
        far,
        in_specs=[in_smem] + [in_vmem] * 2,
    )


def raw_scores(unit, tests, share):
    rows, width = tests[0].shape
    count = len(tests)

    def kernel(unit_ref, *refs):
        every = jnp.concatenate([ref[...] for ref in refs[:count]], axis=0)
        refs[count][...] = inverse_temp * products(every, unit_ref[:share, :])

    return call(
        kernel,
        "raw_scores",
        jax.ShapeDtypeStruct((count * rows, share), jnp.float32),
        2 * count * rows * share * width,
        4 * count * rows * share,
        unit,
        *tests,
        in_specs=[in_vmem] * (1 + count),
    )


def write_scores(bank, raw, keep, received, far, groups, total):
    every, share = raw.shape
    rows, per_row = every // groups, share // lanes

    def kernel(bank_ref, raw_ref, keep_ref, received_ref, far_ref, out_ref, staged, sems):
        normalizer = keep_ref[0:1, :] + received_ref[0:1, :] + far_ref[...]
        shift = jnp.log(normalizer / total)
        copies = []
        for mask in range(groups):
            values = raw_ref[mask * rows : (mask + 1) * rows, :] - shift
            for k in range(per_row):
                staged[mask, pl.ds(k, rows, stride=per_row), :] = values[:, k * lanes : (k + 1) * lanes]
            begin = pl.multiple_of((bank_ref[0] ^ mask) * (rows * per_row), rows * per_row)
            copies.append(
                pltpu.make_async_copy(
                    staged.at[mask], out_ref.at[pl.ds(begin, rows * per_row)], sems.at[mask]
                )
            )
            copies[mask].start()
        for copy in copies:
            copy.wait()

    return call(
        kernel,
        "write_scores",
        jax.ShapeDtypeStruct((every * per_row, lanes), jnp.float32),
        every * share,
        8 * every * share,
        bank,
        raw,
        keep,
        received,
        far,
        in_specs=[in_smem] + [in_vmem] * 4,
        out_specs=in_hbm,
        scratch=[
            pltpu.VMEM((groups, rows * per_row, lanes), jnp.float32),
            pltpu.SemaphoreType.DMA((groups,)),
        ],
    )


def swap(values, axis, mask):
    size = lax.axis_size(axis)
    return lax.ppermute(values, axis, [(i, i ^ mask) for i in range(size)])


def after(values, other):
    return lax.optimization_barrier((values, other))[0]


def local(querybank, gallery, test_queries):
    groups, shards = lax.axis_size("bank"), lax.axis_size("gal")
    rows = querybank.shape[0]
    share = gallery.shape[0] // groups
    bank = lax.axis_index("bank").astype(jnp.int32)[None]
    gal = lax.axis_index("gal").astype(jnp.int32)[None]

    half = shards // 2
    across = normalize(swap(querybank, "gal", half))
    payload = prepare(querybank, test_queries)
    near = [payload] + [swap(payload, "gal", mask) for mask in range(1, half)]

    unit = unit_gallery(bank, gallery, share)
    here = near_tests(gal, [near[0]] + [after(x, across) for x in near[1:]], rows)
    there = swap(here, "gal", half)
    last = [swap(across, "gal", mask) for mask in range(1, half)]
    sums = [first_sums(unit, near, [], rows)]

    sums.append(first_sums(unit, [across, last[0]], [], rows))
    tests = all_tests(gal, here, after(there, sums), half)
    tests_y = swap(tests, "bank", 2)
    tests_core = swap(tests, "bank", 1)
    tests_both = swap(tests_y, "bank", 1)
    raw = raw_scores(unit, [tests, tests_core, tests_y, tests_both], share)

    keep, send = last_sums(unit, [after(last[1], tests), after(last[2], tests)], sums, rows, share)
    received = swap(send, "bank", 2)
    other = swap(keep[1:] + received[1:], "bank", 1)
    result = write_scores(bank, raw, keep, received, other, groups, rows * shards * groups)
    return result.reshape(-1, 1, share)


def solution(mesh):
    placed = (P(("bank", "gal"), None), P("gal", None), P(("bank", "gal"), None))
    return jax.shard_map(
        local, mesh=mesh, in_specs=placed, out_specs=P(None, "gal", "bank"), check_vma=False
    )
```

```python
import jax
import jax.numpy as jnp
from jax import lax
from jax.experimental import pallas as pl
from jax.experimental.pallas import tpu as pltpu
from jax.sharding import PartitionSpec as P

inverse_temp = 20.0
epsilon = 1e-06
log2_e = 1.4426950408889634
lanes = 128
in_vmem = pl.BlockSpec(memory_space=pltpu.VMEM)
in_smem = pl.BlockSpec(memory_space=pltpu.SMEM)
in_hbm = pl.BlockSpec(memory_space=pltpu.HBM)


def unit_rows(values):
    wide = values.astype(jnp.float32)
    return (wide * lax.rsqrt(jnp.sum(wide * wide, axis=-1, keepdims=True) + epsilon)).astype(
        jnp.bfloat16
    )


def products(left, right):
    return lax.dot_general(
        left, right, (((1,), (1,)), ((), ())), preferred_element_type=jnp.float32
    )


def exp_sums(captions, clips):
    grown = jnp.exp2(products(captions, clips) * (inverse_temp * log2_e))
    return jnp.sum(grown.reshape(grown.shape[0] // 8, 8, grown.shape[1]), axis=0)


def all_sums(captions, clips):
    parts = [
        exp_sums(jnp.concatenate(captions[k : k + 4], axis=0), clips) for k in range(0, len(captions), 4)
    ]
    return sum(parts[1:], parts[0])


def call(kernel, name, out_shape, flops, moved, *args, in_specs, out_specs=in_vmem, scratch=()):
    return pl.pallas_call(
        kernel,
        out_shape=out_shape,
        in_specs=in_specs,
        out_specs=out_specs,
        scratch_shapes=list(scratch),
        cost_estimate=pl.CostEstimate(flops=flops, bytes_accessed=moved, transcendentals=0),
        compiler_params=pltpu.CompilerParams(vmem_limit_bytes=32 * 1024 * 1024),
        name=name,
    )(*args)


def stay_in_hbm(values):
    return pltpu.with_memory_space_constraint(values, pltpu.HBM)


def prepare(captions, tests):
    rows, more, width = captions.shape[0], tests.shape[0], captions.shape[1]

    def kernel(captions_ref, tests_ref, out_ref, captions_in, tests_in, sems):
        first = pltpu.make_async_copy(captions_ref, captions_in, sems.at[0])
        second = pltpu.make_async_copy(tests_ref, tests_in, sems.at[1])
        first.start()
        second.start()
        second.wait()
        out_ref[rows:, :] = unit_rows(tests_in[...])
        first.wait()
        out_ref[:rows, :] = unit_rows(captions_in[...])

    return call(
        kernel,
        "prepare",
        jax.ShapeDtypeStruct((rows + more, width), jnp.bfloat16),
        rows * width,
        rows * width * 4,
        stay_in_hbm(captions),
        stay_in_hbm(tests),
        in_specs=[in_hbm] * 2,
        scratch=[
            pltpu.VMEM(captions.shape, captions.dtype),
            pltpu.VMEM(tests.shape, tests.dtype),
            pltpu.SemaphoreType.DMA((2,)),
        ],
    )


def normalize(captions):
    rows, width = captions.shape

    def kernel(captions_ref, out_ref):
        out_ref[...] = unit_rows(captions_ref[...])

    return call(
        kernel,
        "normalize",
        jax.ShapeDtypeStruct((rows, width), jnp.bfloat16),
        10**9,
        4 * rows * width,
        captions,
        in_specs=[in_vmem],
    )


def unit_gallery(bank, gallery, share):
    clips, width = gallery.shape
    quarters = clips // share

    def kernel(bank_ref, gallery_ref, out_ref, arrived, sems):
        half = share // 2
        copies = []
        for k in range(2 * quarters):
            begin = pl.multiple_of(((k // 2) ^ bank_ref[0]) * share + k % 2 * half, half)
            copies.append(
                pltpu.make_async_copy(gallery_ref.at[pl.ds(begin, half)], arrived.at[k], sems.at[k])
            )
            copies[k].start()
        for k in range(2 * quarters):
            copies[k].wait()
            out_ref[k * half : (k + 1) * half, :] = unit_rows(arrived[k])

    return call(
        kernel,
        "unit_gallery",
        jax.ShapeDtypeStruct((clips, width), jnp.bfloat16),
        4 * clips * width,
        4 * clips * width,
        bank,
        stay_in_hbm(gallery),
        in_specs=[in_smem, in_hbm],
        scratch=[
            pltpu.VMEM((2 * quarters, share // 2, width), gallery.dtype),
            pltpu.SemaphoreType.DMA((2 * quarters,)),
        ],
    )


def first_sums(unit, payloads, raw, rows):
    clips, width = unit.shape
    done = len(payloads)
    payloads = payloads + raw
    count = len(payloads)

    def kernel(unit_ref, *refs):
        captions = [ref[:rows, :] for ref in refs[:done]]
        captions += [unit_rows(ref[...]) for ref in refs[done:count]]
        refs[count][...] = all_sums(captions, unit_ref[...])

    return call(
        kernel,
        "first_sums",
        jax.ShapeDtypeStruct((8, clips), jnp.float32),
        2 * rows * clips * width * count,
        2 * clips * width,
        unit,
        *payloads,
        in_specs=[in_vmem] * (count + 1),
    )


def last_sums(unit, raw, sums, rows, share):
    clips, width = unit.shape
    count, parts = len(raw), len(sums)
    half = clips // share // 2

    def kernel(unit_ref, *refs):
        total = all_sums([ref[...] for ref in refs[:count]], unit_ref[...])
        for ref in refs[count : count + parts]:
            total = total + ref[...]
        total = jnp.sum(total, axis=0, keepdims=True)
        keep_ref, send_ref = refs[count + parts :]
        for k in range(half):
            keep_ref[k : k + 1, :] = total[:, k * share : (k + 1) * share]
            send_ref[k : k + 1, :] = total[:, (half + k) * share : (half + k + 1) * share]

    return call(
        kernel,
        "last_sums",
        [jax.ShapeDtypeStruct((half, share), jnp.float32)] * 2,
        2 * rows * clips * width * count,
        2 * clips * width,
        unit,
        *raw,
        *sums,
        in_specs=[in_vmem] * (1 + count + parts),
        out_specs=[in_vmem] * 2,
    )


def near_tests(gal, payloads, rows):
    total, width = payloads[0].shape
    more, count = total - rows, len(payloads)

    def kernel(gal_ref, *refs):
        for mask in range(count):
            place = pl.multiple_of(((gal_ref[0] ^ mask) % count) * more, more)
            refs[count][pl.ds(place, more), :] = refs[mask][rows:, :]

    return call(
        kernel,
        "near_tests",
        jax.ShapeDtypeStruct((count * more, width), jnp.bfloat16),
        0,
        4 * count * more * width,
        gal,
        *payloads,
        in_specs=[in_smem] + [in_vmem] * count,
    )


def all_tests(gal, near, far, near_count):
    rows, width = near.shape

    def kernel(gal_ref, near_ref, far_ref, out_ref):
        half = (gal_ref[0] // near_count) % 2
        out_ref[pl.ds(pl.multiple_of(half * rows, rows), rows), :] = near_ref[...]
        out_ref[pl.ds(pl.multiple_of((1 - half) * rows, rows), rows), :] = far_ref[...]

    return call(
        kernel,
        "all_tests",
        jax.ShapeDtypeStruct((2 * rows, width), jnp.bfloat16),
        0,
        8 * rows * width,
        gal,
        near,
        far,
        in_specs=[in_smem] + [in_vmem] * 2,
    )


def raw_scores(unit, tests, share):
    rows, width = tests[0].shape
    count = len(tests)

    def kernel(unit_ref, *refs):
        every = jnp.concatenate([ref[...] for ref in refs[:count]], axis=0)
        refs[count][...] = inverse_temp * products(every, unit_ref[:share, :])

    return call(
        kernel,
        "raw_scores",
        jax.ShapeDtypeStruct((count * rows, share), jnp.float32),
        2 * count * rows * share * width,
        4 * count * rows * share,
        unit,
        *tests,
        in_specs=[in_vmem] * (1 + count),
    )


def write_scores(bank, raw, keep, received, far, groups, total):
    every, share = raw.shape
    rows, per_row = every // groups, share // lanes

    def kernel(bank_ref, raw_ref, keep_ref, received_ref, far_ref, out_ref, staged, sems):
        normalizer = keep_ref[0:1, :] + received_ref[0:1, :] + far_ref[...]
        shift = jnp.log(normalizer / total)
        copies = []
        for mask in range(groups):
            values = raw_ref[mask * rows : (mask + 1) * rows, :] - shift
            for k in range(per_row):
                staged[mask, pl.ds(k, rows, stride=per_row), :] = values[:, k * lanes : (k + 1) * lanes]
            begin = pl.multiple_of((bank_ref[0] ^ mask) * (rows * per_row), rows * per_row)
            copies.append(
                pltpu.make_async_copy(
                    staged.at[mask], out_ref.at[pl.ds(begin, rows * per_row)], sems.at[mask]
                )
            )
            copies[mask].start()
        for copy in copies:
            copy.wait()

    return call(
        kernel,
        "write_scores",
        jax.ShapeDtypeStruct((every * per_row, lanes), jnp.float32),
        every * share,
        8 * every * share,
        bank,
        raw,
        keep,
        received,
        far,
        in_specs=[in_smem] + [in_vmem] * 4,
        out_specs=in_hbm,
        scratch=[
            pltpu.VMEM((groups, rows * per_row, lanes), jnp.float32),
            pltpu.SemaphoreType.DMA((groups,)),
        ],
    )


def swap(values, axis, mask):
    size = lax.axis_size(axis)
    return lax.ppermute(values, axis, [(i, i ^ mask) for i in range(size)])


def after(values, other):
    return lax.optimization_barrier((values, other))[0]


def local(querybank, gallery, test_queries):
    groups, shards = lax.axis_size("bank"), lax.axis_size("gal")
    rows = querybank.shape[0]
    share = gallery.shape[0] // groups
    bank = lax.axis_index("bank").astype(jnp.int32)[None]
    gal = lax.axis_index("gal").astype(jnp.int32)[None]

    half = shards // 2
    across = normalize(swap(querybank, "gal", half))
    payload = prepare(querybank, test_queries)
    near = [payload] + [swap(payload, "gal", mask) for mask in range(1, half)]

    unit = unit_gallery(bank, gallery, share)
    here = near_tests(gal, [near[0]] + [after(x, across) for x in near[1:]], rows)
    there = swap(here, "gal", half)
    last = [swap(across, "gal", mask) for mask in range(1, half)]
    sums = [first_sums(unit, near, [], rows)]

    sums.append(first_sums(unit, [across, last[0]], [], rows))
    tests = all_tests(gal, here, after(there, sums), half)
    tests_y = swap(tests, "bank", 2)
    tests_core = swap(tests, "bank", 1)
    tests_both = swap(tests_y, "bank", 1)
    raw = raw_scores(unit, [tests, tests_core, tests_y, tests_both], share)

    keep, send = last_sums(unit, [after(came, tests) for came in last[1:]], sums, rows, share)
    received = swap(send, "bank", 2)
    other = swap(keep[1:] + received[1:], "bank", 1)
    result = write_scores(bank, raw, keep, received, other, groups, rows * shards * groups)
    return result.reshape(-1, 1, share)


def solution(mesh):
    placed = (P(("bank", "gal"), None), P("gal", None), P(("bank", "gal"), None))
    return jax.shard_map(
        local, mesh=mesh, in_specs=placed, out_specs=P(None, "gal", "bank"), check_vma=False
    )
```

```python
import jax
import jax.numpy as jnp
from jax import lax
from jax.experimental import pallas as pl
from jax.experimental.pallas import tpu as pltpu
from jax.sharding import PartitionSpec as P

inverse_temp = 20.0
epsilon = 1e-06
log2_e = 1.4426950408889634
lanes = 128
in_vmem = pl.BlockSpec(memory_space=pltpu.VMEM)
in_smem = pl.BlockSpec(memory_space=pltpu.SMEM)
in_hbm = pl.BlockSpec(memory_space=pltpu.HBM)


def unit_rows(values):
    wide = values.astype(jnp.float32)
    return (wide * lax.rsqrt(jnp.sum(wide * wide, axis=-1, keepdims=True) + epsilon)).astype(
        jnp.bfloat16
    )


def products(left, right):
    return lax.dot_general(
        left, right, (((1,), (1,)), ((), ())), preferred_element_type=jnp.float32
    )


def exp_sums(captions, clips):
    grown = jnp.exp2(products(captions, clips) * (inverse_temp * log2_e))
    return jnp.sum(grown.reshape(grown.shape[0] // 8, 8, grown.shape[1]), axis=0)


def all_sums(captions, clips):
    parts = [
        exp_sums(jnp.concatenate(captions[k : k + 4], axis=0), clips) for k in range(0, len(captions), 4)
    ]
    return sum(parts[1:], parts[0])


def call(kernel, name, out_shape, flops, moved, *args, in_specs, out_specs=in_vmem, scratch=()):
    return pl.pallas_call(
        kernel,
        out_shape=out_shape,
        in_specs=in_specs,
        out_specs=out_specs,
        scratch_shapes=list(scratch),
        cost_estimate=pl.CostEstimate(flops=flops, bytes_accessed=moved, transcendentals=0),
        compiler_params=pltpu.CompilerParams(vmem_limit_bytes=32 * 1024 * 1024),
        name=name,
    )(*args)


def stay_in_hbm(values):
    return pltpu.with_memory_space_constraint(values, pltpu.HBM)


def prepare(captions, tests):
    rows, more, width = captions.shape[0], tests.shape[0], captions.shape[1]

    def kernel(captions_ref, tests_ref, out_ref, captions_in, tests_in, sems):
        first = pltpu.make_async_copy(captions_ref, captions_in, sems.at[0])
        second = pltpu.make_async_copy(tests_ref, tests_in, sems.at[1])
        first.start()
        second.start()
        second.wait()
        out_ref[rows:, :] = unit_rows(tests_in[...])
        first.wait()
        out_ref[:rows, :] = unit_rows(captions_in[...])

    return call(
        kernel,
        "prepare",
        jax.ShapeDtypeStruct((rows + more, width), jnp.bfloat16),
        rows * width,
        rows * width * 4,
        stay_in_hbm(captions),
        stay_in_hbm(tests),
        in_specs=[in_hbm] * 2,
        scratch=[
            pltpu.VMEM(captions.shape, captions.dtype),
            pltpu.VMEM(tests.shape, tests.dtype),
            pltpu.SemaphoreType.DMA((2,)),
        ],
    )


def normalize(captions):
    rows, width = captions.shape

    def kernel(captions_ref, out_ref):
        out_ref[...] = unit_rows(captions_ref[...])

    return call(
        kernel,
        "normalize",
        jax.ShapeDtypeStruct((rows, width), jnp.bfloat16),
        10**9,
        4 * rows * width,
        captions,
        in_specs=[in_vmem],
    )


def unit_gallery(bank, gallery, share):
    clips, width = gallery.shape
    quarters = clips // share

    def kernel(bank_ref, gallery_ref, out_ref, arrived, sems):
        half = share // 2
        copies = []
        for k in range(2 * quarters):
            begin = pl.multiple_of(((k // 2) ^ bank_ref[0]) * share + k % 2 * half, half)
            copies.append(
                pltpu.make_async_copy(gallery_ref.at[pl.ds(begin, half)], arrived.at[k], sems.at[k])
            )
            copies[k].start()
        for k in range(2 * quarters):
            copies[k].wait()
            out_ref[k * half : (k + 1) * half, :] = unit_rows(arrived[k])

    return call(
        kernel,
        "unit_gallery",
        jax.ShapeDtypeStruct((clips, width), jnp.bfloat16),
        4 * clips * width,
        4 * clips * width,
        bank,
        stay_in_hbm(gallery),
        in_specs=[in_smem, in_hbm],
        scratch=[
            pltpu.VMEM((2 * quarters, share // 2, width), gallery.dtype),
            pltpu.SemaphoreType.DMA((2 * quarters,)),
        ],
    )


def first_sums(unit, payloads, raw, rows):
    clips, width = unit.shape
    done = len(payloads)
    payloads = payloads + raw
    count = len(payloads)

    def kernel(unit_ref, *refs):
        captions = [ref[:rows, :] for ref in refs[:done]]
        captions += [unit_rows(ref[...]) for ref in refs[done:count]]
        refs[count][...] = all_sums(captions, unit_ref[...])

    return call(
        kernel,
        "first_sums",
        jax.ShapeDtypeStruct((8, clips), jnp.float32),
        2 * rows * clips * width * count,
        2 * clips * width,
        unit,
        *payloads,
        in_specs=[in_vmem] * (count + 1),
    )


def last_sums(unit, raw, sums, rows, share):
    clips, width = unit.shape
    count, parts = len(raw), len(sums)
    half = clips // share // 2

    def kernel(unit_ref, *refs):
        total = all_sums([ref[...] for ref in refs[:count]], unit_ref[...])
        for ref in refs[count : count + parts]:
            total = total + ref[...]
        total = jnp.sum(total, axis=0, keepdims=True)
        keep_ref, send_ref = refs[count + parts :]
        for k in range(half):
            keep_ref[k : k + 1, :] = total[:, k * share : (k + 1) * share]
            send_ref[k : k + 1, :] = total[:, (half + k) * share : (half + k + 1) * share]

    return call(
        kernel,
        "last_sums",
        [jax.ShapeDtypeStruct((half, share), jnp.float32)] * 2,
        2 * rows * clips * width * count,
        2 * clips * width,
        unit,
        *raw,
        *sums,
        in_specs=[in_vmem] * (1 + count + parts),
        out_specs=[in_vmem] * 2,
    )


def near_tests(gal, payloads, rows):
    total, width = payloads[0].shape
    more, count = total - rows, len(payloads)

    def kernel(gal_ref, *refs):
        for mask in range(count):
            place = pl.multiple_of(((gal_ref[0] ^ mask) % count) * more, more)
            refs[count][pl.ds(place, more), :] = refs[mask][rows:, :]

    return call(
        kernel,
        "near_tests",
        jax.ShapeDtypeStruct((count * more, width), jnp.bfloat16),
        0,
        4 * count * more * width,
        gal,
        *payloads,
        in_specs=[in_smem] + [in_vmem] * count,
    )


def all_tests(gal, near, far, near_count):
    rows, width = near.shape

    def kernel(gal_ref, near_ref, far_ref, out_ref):
        half = (gal_ref[0] // near_count) % 2
        out_ref[pl.ds(pl.multiple_of(half * rows, rows), rows), :] = near_ref[...]
        out_ref[pl.ds(pl.multiple_of((1 - half) * rows, rows), rows), :] = far_ref[...]

    return call(
        kernel,
        "all_tests",
        jax.ShapeDtypeStruct((2 * rows, width), jnp.bfloat16),
        0,
        8 * rows * width,
        gal,
        near,
        far,
        in_specs=[in_smem] + [in_vmem] * 2,
    )


def raw_scores(unit, tests, share):
    rows, width = tests[0].shape
    count = len(tests)

    def kernel(unit_ref, *refs):
        every = jnp.concatenate([ref[...] for ref in refs[:count]], axis=0)
        refs[count][...] = inverse_temp * products(every, unit_ref[:share, :])

    return call(
        kernel,
        "raw_scores",
        jax.ShapeDtypeStruct((count * rows, share), jnp.float32),
        2 * count * rows * share * width,
        4 * count * rows * share,
        unit,
        *tests,
        in_specs=[in_vmem] * (1 + count),
    )


def write_scores(bank, raw, keep, received, far, groups, total):
    share = raw[0].shape[1]
    every = raw[0].shape[0] + raw[1].shape[0]
    rows, per_row = every // groups, share // lanes

    def kernel(bank_ref, near_ref, away_ref, keep_ref, received_ref, far_ref, out_ref, staged, sems):
        normalizer = keep_ref[0:1, :] + received_ref[0:1, :] + far_ref[...]
        shift = jnp.log(normalizer / total)
        copies = []
        for mask in range(groups):
            raw_ref, at = (near_ref, mask) if mask < groups // 2 else (away_ref, mask - groups // 2)
            values = raw_ref[at * rows : (at + 1) * rows, :] - shift
            for k in range(per_row):
                staged[mask, pl.ds(k, rows, stride=per_row), :] = values[:, k * lanes : (k + 1) * lanes]
            begin = pl.multiple_of((bank_ref[0] ^ mask) * (rows * per_row), rows * per_row)
            copies.append(
                pltpu.make_async_copy(
                    staged.at[mask], out_ref.at[pl.ds(begin, rows * per_row)], sems.at[mask]
                )
            )
            copies[mask].start()
        for copy in copies:
            copy.wait()

    return call(
        kernel,
        "write_scores",
        jax.ShapeDtypeStruct((every * per_row, lanes), jnp.float32),
        every * share,
        8 * every * share,
        bank,
        *raw,
        keep,
        received,
        far,
        in_specs=[in_smem] + [in_vmem] * 5,
        out_specs=in_hbm,
        scratch=[
            pltpu.VMEM((groups, rows * per_row, lanes), jnp.float32),
            pltpu.SemaphoreType.DMA((groups,)),
        ],
    )


def swap(values, axis, mask):
    size = lax.axis_size(axis)
    return lax.ppermute(values, axis, [(i, i ^ mask) for i in range(size)])


def after(values, other):
    return lax.optimization_barrier((values, other))[0]


def local(querybank, gallery, test_queries):
    groups, shards = lax.axis_size("bank"), lax.axis_size("gal")
    rows = querybank.shape[0]
    share = gallery.shape[0] // groups
    bank = lax.axis_index("bank").astype(jnp.int32)[None]
    gal = lax.axis_index("gal").astype(jnp.int32)[None]

    half = shards // 2
    across = normalize(swap(querybank, "gal", half))
    payload = prepare(querybank, test_queries)
    near = [payload] + [swap(payload, "gal", mask) for mask in range(1, half)]

    unit = unit_gallery(bank, gallery, share)
    here = near_tests(gal, [near[0]] + [after(x, across) for x in near[1:]], rows)
    there = swap(here, "gal", half)
    last = [swap(across, "gal", mask) for mask in range(1, half)]
    sums = [first_sums(unit, near, [], rows)]

    sums.append(first_sums(unit, [across, last[0]], [], rows))
    tests = all_tests(gal, here, after(there, sums), half)
    far = after(there, sums)
    tests_y = all_tests(gal, swap(after(here, sums[0]), "bank", 2), swap(far, "bank", 2), half)
    tests_core = swap(tests, "bank", 1)
    tests_both = swap(tests_y, "bank", 1)
    raw = [raw_scores(unit, [tests, tests_core], share), raw_scores(unit, [tests_y, tests_both], share)]

    keep, send = last_sums(unit, [after(came, tests) for came in last[1:]], sums, rows, share)
    received = swap(send, "bank", 2)
    other = swap(keep[1:] + received[1:], "bank", 1)
    result = write_scores(bank, raw, keep, received, other, groups, rows * shards * groups)
    return result.reshape(-1, 1, share)


def solution(mesh):
    placed = (P(("bank", "gal"), None), P("gal", None), P(("bank", "gal"), None))
    return jax.shard_map(
        local, mesh=mesh, in_specs=placed, out_specs=P(None, "gal", "bank"), check_vma=False
    )
```
